256 devices in a mesh: row: 32 (over y, z), col: 8 (over x, core).
Axes of the slice: x: 4, y: 4, z: 8, core: 2. Of those that a mesh axis runs over, the one named last changes fastest.
Arguments:
- cotangent: float32 [131072, 256], P(('row', 'col')), may hold values from -6 to 6
- out_degree: int32 [131072], P(('row', 'col')), may hold values from 1 to 8
- in_degree: int32 [131072], P(('row', 'col')), may hold values from 1 to 8
- coeffs: float32 [4], replicated, may hold values from 0.3 to 1.2
- tiles: bfloat16 [32, 8, 32, 4, 128, 128], P('row', 'col'), may hold values from -0.75 to 0.75
- pattern: int32 [32, 8, 32, 4], P('row', 'col'), may hold values from 0 to 63, as said below
- requests: int32 [32, 8, 32, 2], P('row', 'col'), may hold values from 0 to 3, as said below
Outputs:
- grad_features: float32 [131072, 256], P(('row', 'col'))
The draws below stay inside these ranges and needn't reach their ends.
Inputs may be any that keep to these rules, and one draw needn't show every extreme that they name: On each device (r, c), every value from 0 to 63 appears in pattern[r, c] at least once. The 2 entries requests[r, c, q, :] are distinct.
All inputs are finite; a program needn't handle non-finite values.
Results may differ from the reference program's by a relative error of at most 0.03.
Values may be sent and summed in bfloat16 or wider, within the bound.
A program may use at most 64 MiB of HBM per device.

```python
import jax
import jax.numpy as jnp
from jax import lax

F = 256
BLK = 128
NB = 4
TPD = 4
CAP = 2
ORDER = 3
DSTB = 32
NBLK = 1024
NODES = 131072
N_ROW = 32
N_COL = 8


def draw_pattern(key, part):
    key = jax.random.fold_in(key, 11)
    keys = jax.random.split(key, N_ROW * N_COL)
    perms = jax.vmap(lambda single: jax.random.permutation(single, DSTB * TPD))(keys)
    return (perms % (N_ROW * CAP)).reshape(N_ROW, N_COL, DSTB, TPD).astype(jnp.int32)


def draw_requests(key, part):
    key = jax.random.fold_in(key, 23)
    scores = jax.random.randint(key, (N_ROW, N_COL, N_ROW, NB), 0, 1 << 20) * NB
    scores = scores + jnp.arange(NB, dtype=jnp.int32)
    ranking = jnp.argsort(scores, axis=-1, stable=True)
    return ranking[..., :CAP].astype(jnp.int32)


def with_ends(array, key, least, top_value):
    index_at = [jax.random.randint(jax.random.fold_in(key, axis), (), 0, length) for axis, length in enumerate(array.shape)]
    longest = array.shape.index(max(array.shape))
    beside = index_at[:longest] + [(index_at[longest] + 1) % array.shape[longest]] + index_at[longest + 1:]
    return array.at[tuple(index_at)].set(least).at[tuple(beside)].set(top_value)


def steps_of(rng, extent, pieces, low, top_value):
    gain, own = 1.0, jax.random.fold_in(rng, 6)
    for axis_at, blocks in pieces:
        steps = jnp.exp(jax.random.uniform(jax.random.fold_in(own, axis_at), (blocks,), jnp.float32, low / len(pieces), top_value / len(pieces)))
        gain = gain * jnp.repeat(steps, extent[axis_at] // blocks).reshape([-1 if axis == axis_at else 1 for axis in range(len(extent))])
    return gain


def normal_values(key, extent, spread, most, shards=(), kind=jnp.bfloat16):
    array = jax.random.normal(key, extent, jnp.float32) * spread
    if len(shards) > 0:
        array = steps_of(key, extent, shards, -0.22, 0.18) * array
    return jnp.clip(array, min=-most, max=most).astype(kind)


def setup_inputs(seed: int = 0) -> dict:
    seeds = jax.random.split(jax.random.key(seed), 8)
    cotangent = normal_values(seeds[0], (NODES, F), 1.0, 6.0, ((0, 256),), jnp.float32)
    out_degree = with_ends(jax.random.randint(seeds[1], (NODES,), 1, 9), jax.random.fold_in(seeds[1], 1), 1, 8).astype(jnp.int32)
    in_degree = with_ends(jax.random.randint(seeds[2], (NODES,), 1, 9), jax.random.fold_in(seeds[2], 1), 1, 8).astype(jnp.int32)
    coeffs = jnp.clip(jax.random.uniform(seeds[3], (ORDER + 1,), jnp.float32, 0.3, 1.2), 0.3, 1.2)
    tiles = normal_values(seeds[4], (N_ROW, N_COL, DSTB, TPD, BLK, BLK), (TPD * BLK // 8) ** -0.5, 0.75, ((0, 32), (1, 8)))
    pattern = draw_pattern(jax.random.fold_in(seeds[7], 71), 0)
    requests = draw_requests(jax.random.fold_in(seeds[7], 71), 0)
    return {"cotangent": cotangent, "out_degree": out_degree, "in_degree": in_degree, "coeffs": coeffs, "tiles": tiles, "pattern": pattern, "requests": requests}


def source_blocks(pattern, requests):
    peer = pattern // CAP
    flat_req = requests.reshape(N_ROW, N_COL, N_ROW * CAP)
    chosen = jnp.take_along_axis(flat_req, pattern.reshape(N_ROW, N_COL, DSTB * TPD), axis=2)
    chosen = chosen.reshape(N_ROW, N_COL, DSTB, TPD)
    column = jnp.arange(N_COL, dtype=jnp.int32)[None, :, None, None]
    return ((peer * N_COL + column) * NB + chosen).astype(jnp.int32)

def reference(cotangent, out_degree, in_degree, coeffs, tiles, pattern, requests):
    src_block = source_blocks(pattern, requests)
    out_scale = lax.rsqrt(out_degree.astype(jnp.float32))[:, None]
    in_scale = lax.rsqrt(in_degree.astype(jnp.float32))[:, None]
    flat_tiles = tiles.reshape(N_ROW * N_COL, DSTB, TPD, BLK, BLK)
    flat_src = src_block.reshape(N_ROW * N_COL, DSTB, TPD)
    h = coeffs[ORDER] * cotangent
    for step in range(ORDER - 1, -1, -1):
        sent = (out_scale * h).astype(jnp.bfloat16).reshape(NBLK, BLK, F)

        def one_device(pair):
            tile_set, sources = pair
            operand = jnp.take(sent, sources.reshape(-1), axis=0).reshape(DSTB, TPD, BLK, F)
            product = jnp.einsum('dtab,dtbf->daf', tile_set.astype(jnp.float32), operand.astype(jnp.float32))
            return product.astype(jnp.bfloat16)
        partial_value = lax.map(one_device, (flat_tiles, flat_src))
        partial_value = partial_value.reshape(N_ROW, N_COL, DSTB * BLK, F).astype(jnp.float32)
        summed = lax.optimization_barrier(jnp.sum(partial_value, axis=1)).reshape(NODES, F)
        h = in_scale * summed + coeffs[step] * cotangent
    return h
```

```python
import functools

import jax
import jax.numpy as jnp
from jax import lax
from jax.experimental import pallas as pl
from jax.experimental.pallas import tpu as pltpu
from jax.sharding import PartitionSpec as P

MESH = pl.DeviceIdType.MESH
BF = jnp.bfloat16
F32 = jnp.float32
Y, Z, X = 4, 8, 4
BLK, NB, TPD, LANES = 128, 4, 4, 128
RA = 96
RB = BLK - RA
SEMS = 50
A1, PY, PZ, A2, SB, XX = 0, 8, 11, 19, 43, 47


def kernel(steps, coef, pat, req, cot, outd, ind, reqv, tiles_hbm, out, *scratch):
    turns = 2 * steps
    za, sa, pk, g1, ss, sr, xs, xr = (scratch[i * turns:(i + 1) * turns] for i in range(8))
    tiles, own, osc, isc, rqv, rqs, gix, ssem, rsem, lsem, qs, qr = scratch[8 * turns:]

    row, col = lax.axis_index("row"), lax.axis_index("col")
    y, z = row // Z, lax.rem(row, Z)
    x, k = col // 2, lax.rem(col, 2)

    def zat(n):
        return lax.rem(z + Z + n, Z)

    def at_z(n):
        return (y * Z + zat(n), col)

    def at_y(n):
        return (lax.rem(y + Y + n, Y) * Z + z, col)

    def at_x(n):
        return (row, lax.rem(x + X + n, X) * 2 + k)

    sibling = (row, x * 2 + 1 - k)
    yoff = (1, -1, 2)

    def remote(t, sem, src, dst, dev):
        return pltpu.make_async_remote_copy(
            src_ref=src, dst_ref=dst, send_sem=ssem.at[t, sem], recv_sem=rsem.at[t, sem], device_id=dev, device_id_type=MESH
        )

    sent = [[] for _ in range(turns)]

    def send(t, sem, src, dst, dev):
        copy = remote(t, sem, src, dst, dev)
        copy.start()
        sent[t].append(copy)

    def arrived(t, sem, dst):
        remote(t, sem, dst, dst, sibling).wait_recv()

    load = pltpu.make_async_copy(tiles_hbm, tiles, lsem.at[0])
    load.start()

    barrier = pltpu.get_barrier_semaphore()
    peers = [at_z(1), at_z(-1), at_y(1), at_y(-1), at_y(2), at_x(1), at_x(-1), at_x(2), sibling]
    for peer in peers:
        pl.semaphore_signal(barrier, inc=1, device_id=peer, device_id_type=MESH)

    for i in range(NB):
        rows = pl.ds(i * BLK, BLK)
        osc[rows] = jnp.transpose(jnp.broadcast_to(lax.rsqrt(outd[i:i + 1].astype(F32)), (BLK, LANES)))
        isc[rows] = jnp.transpose(jnp.broadcast_to(lax.rsqrt(ind[i:i + 1].astype(F32)), (BLK, LANES)))

    pl.semaphore_wait(barrier, len(peers))

    asks = []
    for i, off in enumerate(yoff):
        ask = pltpu.make_async_remote_copy(
            src_ref=reqv, dst_ref=rqv.at[i], send_sem=qs.at[i], recv_sem=qr.at[i], device_id=at_y(-off), device_id_type=MESH
        )
        ask.start()
        asks.append(ask)

    def place(t, i, value):
        za[t][z, i] = value[:RA]
        g1[t][z * 16 + y * 4 + i] = value[RA:]

    def lanes(t):
        return pl.ds((t % 2) * LANES, LANES)

    def pack(t, e, zz):
        blocks = [za[t][zz, i] for i in range(NB)]
        slot = (y * Z + zz) * 2

        def chosen(r):
            return jnp.where(r == 0, blocks[0], jnp.where(r == 1, blocks[1], jnp.where(r == 2, blocks[2], blocks[3])))

        for i, off in enumerate(yoff):
            for s in range(2):
                pk[t][e, i, s] = chosen(rqs[i, 0, slot + s])
            send(t, A2 + e * 3 + i, pk[t].at[e, i], sa[t].at[pl.ds(slot, 2)], at_y(off))
        for s in range(2):
            sa[t][slot + s] = chosen(req[slot + s])

    def whole(t, zz):
        return za[t].at[zz]

    def column(t, zz):
        return g1[t].at[pl.ds(zz * 16, 16)]

    def start(t):
        mine = g1[t].at[pl.ds(z * 16 + y * 4, 4)]
        send(t, A1, whole(t, z), whole(t, z), at_z(1))
        send(t, A1 + 4, whole(t, z), whole(t, z), at_z(-1))
        for i, off in enumerate(yoff):
            send(t, PY + i, mine, mine, at_y(off))

    def gather(t):
        pack(t, 0, z)
        yield
        e = 1
        for hop in range(1, 5):
            if hop < 4:
                for d, sign in enumerate((-1, 1)):
                    zz = zat(sign * hop)
                    arrived(t, A1 + d * 4 + hop - 1, whole(t, zz))
                    if hop < 3:
                        part = whole(t, zz)
                    else:
                        part = za[t].at[zz, pl.ds(2 * d, 2)]
                    send(t, A1 + d * 4 + hop, part, part, at_z(-sign))
                for sign in (-1, 1):
                    pack(t, e, zat(sign * hop))
                    e += 1
            else:
                zz = zat(4)
                for d in range(2):
                    arrived(t, A1 + d * 4 + 3, za[t].at[zz, pl.ds(2 * d, 2)])
                pack(t, e, zz)
            yield
            if hop == 1:
                for i, off in enumerate(yoff):
                    yy = lax.rem(y + Y - off, Y)
                    arrived(t, PY + i, g1[t].at[pl.ds(z * 16 + yy * 4, 4)])
                for d, sign in enumerate((-1, 1)):
                    send(t, PZ + d * 4, column(t, z), column(t, z), at_z(-sign))
            else:
                for d, sign in enumerate((-1, 1)):
                    zz = zat(sign * (hop - 1))
                    arrived(t, PZ + d * 4 + hop - 2, column(t, zz))
                    if hop < 4:
                        part = column(t, zz)
                    else:
                        part = g1[t].at[pl.ds(zz * 16 + 8 * d, 8)]
                    send(t, PZ + d * 4 + hop - 1, part, part, at_z(-sign))
            yield
        for d in range(2):
            arrived(t, PZ + d * 4 + 3, g1[t].at[pl.ds(zat(4) * 16 + 8 * d, 8)])
        order = [z] + [zat(sign * hop) for hop in (1, 2, 3) for sign in (-1, 1)] + [zat(4)]
        for e, zz in enumerate(order):
            for i, off in enumerate(yoff):
                yy = lax.rem(y + Y - off, Y)
                arrived(t, A2 + e * 3 + i, sa[t].at[pl.ds((yy * Z + zz) * 2, 2)])

    def product(t, d):
        left = jnp.concatenate([tiles[d, j] for j in range(TPD)], axis=1)
        right = []
        for j in range(TPD):
            p = pat[d * TPD + j]
            right += [sa[t][p], g1[t][gix[d * TPD + j]]]
        return jnp.dot(left, jnp.concatenate(right, axis=0), preferred_element_type=F32)

    def reduce(t):
        def for_sibling(n, carry):
            to = lax.rem(x + n + 1, X) * 2 + 1 - k
            for i in range(NB):
                ss[t][n, i] = product(t, to * NB + i).astype(BF)
            remote(t, SB + n, ss[t].at[n], sr[t].at[n], sibling).start()
            return carry

        lax.fori_loop(0, 2, for_sibling, 0)
        yield
        lax.fori_loop(2, 4, for_sibling, 0)
        yield

        def for_x(n, carry):
            to = lax.rem(x + n + 1, X) * 2 + k
            sums = [product(t, to * NB + i) for i in range(NB)]
            arrived(t, SB + n, sr[t].at[n])
            for i in range(NB):
                xs[t][n, i] = (sums[i] + sr[t][n, i].astype(F32)).astype(BF)
            remote(t, XX + n, xs[t].at[n], xr[t].at[n], at_x(n + 1)).start()
            return carry

        lax.fori_loop(0, 3, for_x, 0)
        yield
        for i in range(NB):
            own[i] = product(t, col * NB + i)
        yield
        arrived(t, SB + 3, sr[t].at[3])
        for n in range(3):
            arrived(t, XX + n, xr[t].at[n])
        level = steps - 1 - t // 2
        for i in range(NB):
            rows = pl.ds(i * BLK, BLK)
            total = own[i] + sr[t][3, i].astype(F32)
            for n in range(3):
                total = total + xr[t][n, i].astype(F32)
            h = isc[rows] * total + coef[level] * cot[rows, lanes(t)]
            if level == 0:
                out[rows, lanes(t)] = h
            else:
                place(t + 2, i, (osc[rows] * h).astype(BF))
        if level > 0:
            start(t + 2)
        for n in range(4):
            remote(t, SB + n, ss[t].at[n], sr[t].at[n], sibling).wait_send()
        for n in range(3):
            remote(t, XX + n, xs[t].at[n], xr[t].at[n], at_x(n + 1)).wait_send()
        yield

    for t in range(2):
        for i in range(NB):
            rows = pl.ds(i * BLK, BLK)
            place(t, i, (osc[rows] * (coef[steps] * cot[rows, lanes(t)])).astype(BF))
        start(t)

    def slot_of(i, carry):
        p = pat[i]
        gix[i] = ((p // 2 % Z) * Y + p // 16) * NB + req[p]
        return carry

    lax.fori_loop(0, gix.shape[0], slot_of, 0)
    for ask in asks:
        ask.wait()
    to_scalar = pltpu.make_async_copy(rqv, rqs, lsem.at[1])
    to_scalar.start()
    to_scalar.wait()

    sums = None
    for t in range(turns):
        events = gather(t)
        live = True
        while live:
            if sums is not None and next(sums, 0) == 0:
                sums = None
            live = next(events, 0) != 0
        while sums is not None and next(sums, 0) != 0:
            pass
        if t == 0:
            load.wait()
        sums = reduce(t)
        if t > 0:
            for copy in sent[t - 1]:
                copy.wait_send()
    for _ in sums:
        pass
    for copy in sent[turns - 1]:
        copy.wait_send()


def on_device(cotangent, out_degree, in_degree, coeffs, tiles, pattern, requests):
    steps = coeffs.shape[0] - 1
    turns = 2 * steps
    ask = requests.reshape(-1)
    shapes = [
        (Z, NB, RA, LANES),
        (Y * Z * 2, RA, LANES),
        (Z, 3, 2, RA, LANES),
        (Y * Z * NB, RB, LANES),
        (4, NB, BLK, LANES),
        (4, NB, BLK, LANES),
        (3, NB, BLK, LANES),
        (3, NB, BLK, LANES),
    ]
    smem, vmem = pl.BlockSpec(memory_space=pltpu.SMEM), pl.BlockSpec(memory_space=pltpu.VMEM)
    return pl.pallas_call(
        functools.partial(kernel, steps),
        out_shape=jax.ShapeDtypeStruct(cotangent.shape, F32),
        in_specs=[smem, smem, smem, vmem, vmem, vmem, vmem, pl.BlockSpec(memory_space=pl.ANY)],
        out_specs=vmem,
        scratch_shapes=[pltpu.VMEM(shape, BF) for shape in shapes for _ in range(turns)]
        + [
            pltpu.VMEM((32, TPD, BLK, BLK), BF),
            pltpu.VMEM((NB, BLK, LANES), F32),
            pltpu.VMEM((NB * BLK, LANES), F32),
            pltpu.VMEM((NB * BLK, LANES), F32),
            pltpu.VMEM((3, 8, 128), jnp.int32),
            pltpu.SMEM((3, 8, 128), jnp.int32),
            pltpu.SMEM((128,), jnp.int32),
            pltpu.SemaphoreType.DMA((turns, SEMS)),
            pltpu.SemaphoreType.DMA((turns, SEMS)),
            pltpu.SemaphoreType.DMA((2,)),
            pltpu.SemaphoreType.DMA((3,)),
            pltpu.SemaphoreType.DMA((3,)),
        ],
        compiler_params=pltpu.CompilerParams(collective_id=0, has_side_effects=True, vmem_limit_bytes=60 << 20),
    )(
        coeffs,
        pattern.reshape(-1),
        ask,
        cotangent,
        out_degree.reshape(NB, BLK),
        in_degree.reshape(NB, BLK),
        jnp.pad(ask.reshape(1, -1), ((0, 7), (0, 128 - ask.shape[0]))),
        tiles[0, 0],
    )


def solution(mesh):
    return jax.shard_map(
        on_device,
        mesh=mesh,
        in_specs=(
            P(("row", "col"), None),
            P(("row", "col")),
            P(("row", "col")),
            P(),
            P("row", "col", None, None, None, None),
            P("row", "col", None, None),
            P("row", "col", None, None),
        ),
        out_specs=P(("row", "col"), None),
        check_vma=False,
    )
```

```python
import functools

import jax
import jax.numpy as jnp
from jax import lax
from jax.experimental import pallas as pl
from jax.experimental.pallas import tpu as pltpu
from jax.sharding import PartitionSpec as P

MESH = pl.DeviceIdType.MESH
BF = jnp.bfloat16
F32 = jnp.float32
Y, Z, X = 4, 8, 4
BLK, NB, TPD, LANES = 128, 4, 4, 128
RA = 96
RB = BLK - RA
SEMS = 50
EVENTS = 20
LEAD = 8
ORDER = "RRggRggRgggRnRgnnn"
A1, PY, PZ, A2, SB, XX = 0, 8, 11, 19, 43, 47


def kernel(steps, coef, pat, req, cot, outd, ind, reqv, tiles_hbm, out, *scratch):
    turns = 2 * steps
    za, sa, pk, g1, ss, sr, xs, xr = (scratch[i * turns:(i + 1) * turns] for i in range(8))
    tiles, own, osc, isc, rqv, rqs, gix, ssem, rsem, lsem, qs, qr = scratch[8 * turns:]

    row, col = lax.axis_index("row"), lax.axis_index("col")
    y, z = row // Z, lax.rem(row, Z)
    x, k = col // 2, lax.rem(col, 2)

    def zat(n):
        return lax.rem(z + Z + n, Z)

    def at_z(n):
        return (y * Z + zat(n), col)

    def at_y(n):
        return (lax.rem(y + Y + n, Y) * Z + z, col)

    def at_x(n):
        return (row, lax.rem(x + X + n, X) * 2 + k)

    sibling = (row, x * 2 + 1 - k)
    yoff = (1, -1, 2)

    def remote(t, sem, src, dst, dev):
        return pltpu.make_async_remote_copy(
            src_ref=src, dst_ref=dst, send_sem=ssem.at[t, sem], recv_sem=rsem.at[t, sem], device_id=dev, device_id_type=MESH
        )

    sent = [[] for _ in range(turns)]

    def send(t, sem, src, dst, dev):
        copy = remote(t, sem, src, dst, dev)
        copy.start()
        sent[t].append(copy)

    def arrived(t, sem, dst):
        remote(t, sem, dst, dst, sibling).wait_recv()

    load = pltpu.make_async_copy(tiles_hbm, tiles, lsem.at[0])
    load.start()

    barrier = pltpu.get_barrier_semaphore()
    peers = [at_z(1), at_z(-1), at_y(1), at_y(-1), at_y(2), at_x(1), at_x(-1), at_x(2), sibling]
    for peer in peers:
        pl.semaphore_signal(barrier, inc=1, device_id=peer, device_id_type=MESH)

    for i in range(NB):
        rows = pl.ds(i * BLK, BLK)
        osc[rows] = jnp.transpose(jnp.broadcast_to(lax.rsqrt(outd[i:i + 1].astype(F32)), (BLK, LANES)))
        isc[rows] = jnp.transpose(jnp.broadcast_to(lax.rsqrt(ind[i:i + 1].astype(F32)), (BLK, LANES)))

    pl.semaphore_wait(barrier, len(peers))

    asks = []
    for i, off in enumerate(yoff):
        ask = pltpu.make_async_remote_copy(
            src_ref=reqv, dst_ref=rqv.at[i], send_sem=qs.at[i], recv_sem=qr.at[i], device_id=at_y(-off), device_id_type=MESH
        )
        ask.start()
        asks.append(ask)

    def place(t, i, value):
        za[t][z, i] = value[:RA]
        g1[t][z * 16 + y * 4 + i] = value[RA:]

    def lanes(t):
        return pl.ds((t % 2) * LANES, LANES)

    def pack(t, e, zz):
        blocks = [za[t][zz, i] for i in range(NB)]
        slot = (y * Z + zz) * 2

        def chosen(r):
            return jnp.where(r == 0, blocks[0], jnp.where(r == 1, blocks[1], jnp.where(r == 2, blocks[2], blocks[3])))

        for i, off in enumerate(yoff):
            for s in range(2):
                pk[t][e, i, s] = chosen(rqs[i, s, y * Z + zz])
            send(t, A2 + e * 3 + i, pk[t].at[e, i], sa[t].at[pl.ds(slot, 2)], at_y(off))
        for s in range(2):
            sa[t][slot + s] = chosen(req[s, y * Z + zz])

    def whole(t, zz):
        return za[t].at[zz]

    def column(t, zz):
        return g1[t].at[pl.ds(zz * 16, 16)]

    def start(t):
        mine = g1[t].at[pl.ds(z * 16 + y * 4, 4)]
        send(t, A1, whole(t, z), whole(t, z), at_z(1))
        send(t, A1 + 4, whole(t, z), whole(t, z), at_z(-1))
        for i, off in enumerate(yoff):
            send(t, PY + i, mine, mine, at_y(off))

    def gather(t):
        pack(t, 0, z)
        yield
        e = 1
        for hop in range(1, 5):
            if hop < 4:
                for d, sign in enumerate((-1, 1)):
                    zz = zat(sign * hop)
                    arrived(t, A1 + d * 4 + hop - 1, whole(t, zz))
                    if hop < 3:
                        part = whole(t, zz)
                    else:
                        part = za[t].at[zz, pl.ds(2 * d, 2)]
                    send(t, A1 + d * 4 + hop, part, part, at_z(-sign))
                yield
                for sign in (-1, 1):
                    pack(t, e, zat(sign * hop))
                    e += 1
            else:
                zz = zat(4)
                for d in range(2):
                    arrived(t, A1 + d * 4 + 3, za[t].at[zz, pl.ds(2 * d, 2)])
                pack(t, e, zz)
            yield
            if hop == 1:
                for i, off in enumerate(yoff):
                    yy = lax.rem(y + Y - off, Y)
                    arrived(t, PY + i, g1[t].at[pl.ds(z * 16 + yy * 4, 4)])
                for d, sign in enumerate((-1, 1)):
                    send(t, PZ + d * 4, column(t, z), column(t, z), at_z(-sign))
            else:
                for d, sign in enumerate((-1, 1)):
                    zz = zat(sign * (hop - 1))
                    arrived(t, PZ + d * 4 + hop - 2, column(t, zz))
                    if hop < 4:
                        part = column(t, zz)
                    else:
                        part = g1[t].at[pl.ds(zz * 16 + 8 * d, 8)]
                    send(t, PZ + d * 4 + hop - 1, part, part, at_z(-sign))
            yield
        for d in range(2):
            arrived(t, PZ + d * 4 + 3, g1[t].at[pl.ds(zat(4) * 16 + 8 * d, 8)])
        yield
        order = [z] + [zat(sign * hop) for hop in (1, 2, 3) for sign in (-1, 1)] + [zat(4)]
        for e, zz in enumerate(order):
            for i, off in enumerate(yoff):
                yy = lax.rem(y + Y - off, Y)
                arrived(t, A2 + e * 3 + i, sa[t].at[pl.ds((yy * Z + zz) * 2, 2)])

    def product(t, d):
        left = jnp.concatenate([tiles[d, j] for j in range(TPD)], axis=1)
        right = []
        for j in range(TPD):
            p = pat[j, d]
            right += [sa[t][p], g1[t][gix[d * TPD + j]]]
        return jnp.dot(left, jnp.concatenate(right, axis=0), preferred_element_type=F32)

    def reduce(t):
        def for_sibling(n, carry):
            to = lax.rem(x + n + 1, X) * 2 + 1 - k
            for i in range(NB):
                ss[t][n, i] = product(t, to * NB + i).astype(BF)
            remote(t, SB + n, ss[t].at[n], sr[t].at[n], sibling).start()
            return carry

        lax.fori_loop(0, 2, for_sibling, 0)
        yield
        lax.fori_loop(2, 4, for_sibling, 0)
        yield

        def for_x(n, carry):
            to = lax.rem(x + n + 1, X) * 2 + k
            sums = [product(t, to * NB + i) for i in range(NB)]
            arrived(t, SB + n, sr[t].at[n])
            for i in range(NB):
                xs[t][n, i] = (sums[i] + sr[t][n, i].astype(F32)).astype(BF)
            remote(t, XX + n, xs[t].at[n], xr[t].at[n], at_x(n + 1)).start()
            return carry

        lax.fori_loop(0, 3, for_x, 0)
        yield
        for i in range(NB):
            own[i] = product(t, col * NB + i)
        yield
        arrived(t, SB + 3, sr[t].at[3])
        for n in range(3):
            arrived(t, XX + n, xr[t].at[n])
        level = steps - 1 - t // 2
        for i in range(NB):
            rows = pl.ds(i * BLK, BLK)
            total = own[i] + sr[t][3, i].astype(F32)
            for n in range(3):
                total = total + xr[t][n, i].astype(F32)
            h = isc[rows] * total + coef[level] * cot[rows, lanes(t)]
            if level == 0:
                out[rows, lanes(t)] = h
            else:
                place(t + 2, i, (osc[rows] * h).astype(BF))
        if level > 0:
            start(t + 2)
        for n in range(4):
            remote(t, SB + n, ss[t].at[n], sr[t].at[n], sibling).wait_send()
        for n in range(3):
            remote(t, XX + n, xs[t].at[n], xr[t].at[n], at_x(n + 1)).wait_send()
        yield

    for t in range(2):
        for i in range(NB):
            rows = pl.ds(i * BLK, BLK)
            place(t, i, (osc[rows] * (coef[steps] * cot[rows, lanes(t)])).astype(BF))
        if t == 0:
            start(t)

    def slot_of(i, carry):
        for j in range(TPD):
            p = pat[j, i]
            gix[i * TPD + j] = ((p // 2 % Z) * Y + p // 16) * NB + req[p % 2, p // 2]
        return carry

    lax.fori_loop(0, pat.shape[1], slot_of, 0)
    for ask in asks:
        ask.wait()
    to_scalar = pltpu.make_async_copy(rqv, rqs, lsem.at[1])
    to_scalar.start()
    to_scalar.wait()

    def run(events, count):
        for _ in range(count):
            next(events, None)

    def settle(t):
        for copy in sent[t]:
            copy.wait_send()

    gathers = {t: gather(t) for t in range(turns)}
    run(gathers[0], LEAD)
    start(1)
    run(gathers[0], EVENTS)
    load.wait()
    for t in range(1, turns + 1):
        streams = {"R": reduce(t - 1), "g": gathers.get(t, iter(())), "n": gathers.get(t + 1, iter(()))}
        for letter in ORDER:
            run(streams[letter], 1)
        run(streams["R"], EVENTS)
        run(streams["g"], EVENTS)
        settle(t - 1)


def on_device(cotangent, out_degree, in_degree, coeffs, tiles, pattern, requests):
    steps = coeffs.shape[0] - 1
    turns = 2 * steps
    ask = requests[0, 0].T
    shapes = [
        (Z, NB, RA, LANES),
        (Y * Z * 2, RA, LANES),
        (Z, 3, 2, RA, LANES),
        (Y * Z * NB, RB, LANES),
        (4, NB, BLK, LANES),
        (4, NB, BLK, LANES),
        (3, NB, BLK, LANES),
        (3, NB, BLK, LANES),
    ]
    smem, vmem = pl.BlockSpec(memory_space=pltpu.SMEM), pl.BlockSpec(memory_space=pltpu.VMEM)
    return pl.pallas_call(
        functools.partial(kernel, steps),
        out_shape=jax.ShapeDtypeStruct(cotangent.shape, F32),
        in_specs=[smem, smem, smem, vmem, vmem, vmem, vmem, pl.BlockSpec(memory_space=pl.ANY)],
        out_specs=vmem,
        scratch_shapes=[pltpu.VMEM(shape, BF) for shape in shapes for _ in range(turns)]
        + [
            pltpu.VMEM((32, TPD, BLK, BLK), BF),
            pltpu.VMEM((NB, BLK, LANES), F32),
            pltpu.VMEM((NB * BLK, LANES), F32),
            pltpu.VMEM((NB * BLK, LANES), F32),
            pltpu.VMEM((3, 2, 32), jnp.int32),
            pltpu.SMEM((3, 2, 32), jnp.int32),
            pltpu.SMEM((128,), jnp.int32),
            pltpu.SemaphoreType.DMA((turns, SEMS)),
            pltpu.SemaphoreType.DMA((turns, SEMS)),
            pltpu.SemaphoreType.DMA((2,)),
            pltpu.SemaphoreType.DMA((3,)),
            pltpu.SemaphoreType.DMA((3,)),
        ],
        compiler_params=pltpu.CompilerParams(collective_id=0, has_side_effects=True, vmem_limit_bytes=60 << 20),
    )(
        coeffs,
        pattern[0, 0].T,
        ask,
        cotangent,
        out_degree.reshape(NB, BLK),
        in_degree.reshape(NB, BLK),
        ask,
        tiles[0, 0],
    )


def solution(mesh):
    return jax.shard_map(
        on_device,
        mesh=mesh,
        in_specs=(
            P(("row", "col"), None),
            P(("row", "col")),
            P(("row", "col")),
            P(),
            P("row", "col", None, None, None, None),
            P("row", "col", None, None),
            P("row", "col", None, None),
        ),
        out_specs=P(("row", "col"), None),
        check_vma=False,
    )
```

```python
import functools

import jax
import jax.numpy as jnp
from jax import lax
from jax.experimental import pallas as pl
from jax.experimental.pallas import tpu as pltpu
from jax.sharding import PartitionSpec as P

MESH = pl.DeviceIdType.MESH
BF = jnp.bfloat16
F32 = jnp.float32
Y, Z, X = 4, 8, 4
BLK, NB, TPD, LANES = 128, 4, 4, 128
RA = 96
RB = BLK - RA
SENDS, ARRIVALS = 6, 21
EVENTS = 40
LEAD = 7
ORDERS = (
    "RggggRgRggRggggRggggRgnRgggnnnngnR",
    "RRggRgRggggRgggggRgnRggnRnnnn",
    "RnRgRggngRggggggngRgnnRnngngnnnnR",
)
A1, PZ, SB, PY, A2, XX = 0, 7, 14, 18, 19, 20
KINDS = {A1: 0, PZ: 1, SB: 2, PY: 3, A2: 4, XX: 5}


def kernel(steps, coef, pat, req, cot, outd, ind, reqv, tiles_hbm, out, *scratch):
    turns = 2 * steps
    za, sa, pk, g1, ss, sr, xs, xr = (scratch[i * turns:(i + 1) * turns] for i in range(8))
    tiles, own, osc, isc, rqv, rqs, gix, ssem, rsem, lsem, qs, qr = scratch[8 * turns:]

    row, col = lax.axis_index("row"), lax.axis_index("col")
    y, z = row // Z, lax.rem(row, Z)
    x, k = col // 2, lax.rem(col, 2)

    def zat(n):
        return lax.rem(z + Z + n, Z)

    def at_z(n):
        return (y * Z + zat(n), col)

    def at_y(n):
        return (lax.rem(y + Y + n, Y) * Z + z, col)

    def at_x(n):
        return (row, lax.rem(x + X + n, X) * 2 + k)

    sibling = (row, x * 2 + 1 - k)
    yoff = (1, -1, 2)

    def remote(t, kind, n, src, dst, dev):
        return pltpu.make_async_remote_copy(
            src_ref=src,
            dst_ref=dst,
            send_sem=ssem.at[t, KINDS[kind]],
            recv_sem=rsem.at[t, kind + n],
            device_id=dev,
            device_id_type=MESH,
        )

    def send(t, kind, n, src, dst, dev):
        remote(t, kind, n, src, dst, dev).start()

    def arrived(t, kind, n, dst):
        remote(t, kind, n, dst, dst, sibling).wait_recv()

    def settle(t):
        for kind, ref in (
            (A1, za[t].at[pl.ds(0, Z - 1)]),
            (PZ, g1[t].at[pl.ds(0, (Z - 1) * Y * NB)]),
            (SB, ss[t]),
            (PY, g1[t].at[pl.ds(0, (Y - 1) * NB)]),
            (A2, pk[t]),
            (XX, xs[t]),
        ):
            remote(t, kind, 0, ref, ref, sibling).wait_send()

    load = pltpu.make_async_copy(tiles_hbm, tiles, lsem.at[0])
    load.start()

    barrier = pltpu.get_barrier_semaphore()
    peers = [at_z(1), at_z(-1), at_y(1), at_y(-1), at_y(2), at_x(1), at_x(-1), at_x(2), sibling]
    for peer in peers:
        pl.semaphore_signal(barrier, inc=1, device_id=peer, device_id_type=MESH)

    for i in range(NB):
        rows = pl.ds(i * BLK, BLK)
        osc[rows] = jnp.transpose(jnp.broadcast_to(lax.rsqrt(outd[i:i + 1].astype(F32)), (BLK, LANES)))
        isc[rows] = jnp.transpose(jnp.broadcast_to(lax.rsqrt(ind[i:i + 1].astype(F32)), (BLK, LANES)))

    pl.semaphore_wait(barrier, len(peers))

    asks = []
    for i, off in enumerate(yoff):
        ask = pltpu.make_async_remote_copy(
            src_ref=reqv, dst_ref=rqv.at[i], send_sem=qs.at[i], recv_sem=qr.at[i], device_id=at_y(-off), device_id_type=MESH
        )
        ask.start()
        asks.append(ask)

    placed = set()

    def place(t, i, value):
        placed.add(t)
        za[t][z, i] = value[:RA]
        g1[t][z * 16 + y * 4 + i] = value[RA:]

    def lanes(t):
        return pl.ds((t % 2) * LANES, LANES)

    def pack(t, e, zz):
        blocks = [za[t][zz, i] for i in range(NB)]
        slot = (y * Z + zz) * 2

        def chosen(r):
            return jnp.where(r == 0, blocks[0], jnp.where(r == 1, blocks[1], jnp.where(r == 2, blocks[2], blocks[3])))

        for i, off in enumerate(yoff):
            for s in range(2):
                pk[t][e, i, s] = chosen(rqs[i, s, y * Z + zz])
            send(t, A2, 0, pk[t].at[e, i], sa[t].at[pl.ds(slot, 2)], at_y(off))
        for s in range(2):
            sa[t][slot + s] = chosen(req[s, y * Z + zz])

    def whole(t, zz):
        return za[t].at[zz]

    def column(t, zz):
        return g1[t].at[pl.ds(zz * 16, 16)]

    def start(t):
        mine = g1[t].at[pl.ds(z * 16 + y * 4, 4)]
        send(t, A1, 0, whole(t, z), whole(t, z), at_z(1))
        send(t, A1, 1, whole(t, z), whole(t, z), at_z(-1))
        for i, off in enumerate(yoff):
            send(t, PY, 0, mine, mine, at_y(off))

    def gather(t):
        assert t in placed
        pack(t, 0, z)
        yield
        e = 1
        for hop in range(1, 5):
            if hop < 4:
                for d, sign in enumerate((-1, 1)):
                    zz = zat(sign * hop)
                    arrived(t, A1, 2 * hop - 2 + d, whole(t, zz))
                    if hop < 3:
                        part = whole(t, zz)
                    else:
                        part = za[t].at[zz, pl.ds(2 * d, 2)]
                    send(t, A1, min(2 * hop + d, 6), part, part, at_z(-sign))
                    yield
                for sign in (-1, 1):
                    pack(t, e, zat(sign * hop))
                    e += 1
                    if sign < 0:
                        yield
            else:
                zz = zat(4)
                arrived(t, A1, 6, whole(t, zz))
                pack(t, e, zz)
            yield
            if hop == 1:
                arrived(t, PY, 0, g1[t].at[pl.ds(0, (Y - 1) * NB)])
                for d, sign in enumerate((-1, 1)):
                    send(t, PZ, d, column(t, z), column(t, z), at_z(-sign))
            else:
                for d, sign in enumerate((-1, 1)):
                    zz = zat(sign * (hop - 1))
                    arrived(t, PZ, 2 * hop - 4 + d, column(t, zz))
                    if hop < 4:
                        part = column(t, zz)
                    else:
                        part = g1[t].at[pl.ds(zz * 16 + 8 * d, 8)]
                    send(t, PZ, min(2 * hop - 2 + d, 6), part, part, at_z(-sign))
                    if d == 0:
                        yield
            yield
        arrived(t, PZ, 6, column(t, zat(4)))
        yield
        arrived(t, A2, 0, sa[t].at[pl.ds(0, (Y - 1) * Z * 2)])

    def product(t, d):
        left = jnp.concatenate([tiles[d, j] for j in range(TPD)], axis=1)
        right = []
        for j in range(TPD):
            p = pat[j, d]
            right += [sa[t][p], g1[t][gix[d * TPD + j]]]
        return jnp.dot(left, jnp.concatenate(right, axis=0), preferred_element_type=F32)

    def reduce(t):
        def for_sibling(n, off):
            to = lax.rem(x + off, X) * 2 + 1 - k
            for i in range(NB):
                ss[t][n, i] = product(t, to * NB + i).astype(BF)
            send(t, SB, n, ss[t].at[n], sr[t].at[n], sibling)

        def for_x(n, off):
            to = lax.rem(x + off, X) * 2 + k
            sums = [product(t, to * NB + i) for i in range(NB)]
            arrived(t, SB, n, sr[t].at[n])
            for i in range(NB):
                xs[t][n, i] = (sums[i] + sr[t][n, i].astype(F32)).astype(BF)
            send(t, XX, 0, xs[t].at[n], xr[t].at[n], at_x(off))

        def first_two(n, carry):
            for_sibling(n, 2 - n)
            return carry

        def last_two(n, carry):
            for_sibling(n, 9 - 3 * n)
            return carry

        def neighbours(n, carry):
            for_x(n, 2 * n - 1)
            return carry

        lax.fori_loop(0, 2, first_two, 0)
        yield
        for_x(0, 2)
        yield
        lax.fori_loop(2, 4, last_two, 0)
        yield
        lax.fori_loop(1, 3, neighbours, 0)
        yield
        for i in range(NB):
            own[i] = product(t, col * NB + i)
        yield
        arrived(t, SB, 3, sr[t].at[3])
        arrived(t, XX, 0, xr[t])
        level = steps - 1 - t // 2
        for i in range(NB):
            rows = pl.ds(i * BLK, BLK)
            total = own[i] + sr[t][3, i].astype(F32)
            for n in range(3):
                total = total + xr[t][n, i].astype(F32)
            h = isc[rows] * total + coef[level] * cot[rows, lanes(t)]
            if level == 0:
                out[rows, lanes(t)] = h
            else:
                place(t + 2, i, (osc[rows] * h).astype(BF))
        if level > 0:
            start(t + 2)
        yield

    for t in range(2):
        for i in range(NB):
            rows = pl.ds(i * BLK, BLK)
            place(t, i, (osc[rows] * (coef[steps] * cot[rows, lanes(t)])).astype(BF))
        if t == 0:
            start(t)

    def slot_of(i, carry):
        for j in range(TPD):
            p = pat[j, i]
            gix[i * TPD + j] = ((p // 2 % Z) * Y + p // 16) * NB + req[p % 2, p // 2]
        return carry

    lax.fori_loop(0, pat.shape[1], slot_of, 0)
    for ask in asks:
        ask.wait()
    to_scalar = pltpu.make_async_copy(rqv, rqs, lsem.at[1])
    to_scalar.start()
    to_scalar.wait()

    def run(events, count):
        for _ in range(count):
            next(events, None)

    gathers = {t: gather(t) for t in range(turns)}
    run(gathers[0], LEAD)
    start(1)
    run(gathers[0], EVENTS)
    load.wait()
    for t in range(1, turns + 1):
        streams = {"R": reduce(t - 1), "g": gathers.get(t, iter(())), "n": gathers.get(t + 1, iter(()))}
        for letter in ORDERS[0 if t == 1 else 1 if t < turns - 1 else 2]:
            run(streams[letter], 1)
        run(streams["R"], EVENTS)
        run(streams["g"], EVENTS)
        settle(t - 1)


def on_device(cotangent, out_degree, in_degree, coeffs, tiles, pattern, requests):
    steps = coeffs.shape[0] - 1
    turns = 2 * steps
    ask = requests[0, 0].T
    shapes = [
        (Z, NB, RA, LANES),
        (Y * Z * 2, RA, LANES),
        (Z, 3, 2, RA, LANES),
        (Y * Z * NB, RB, LANES),
        (4, NB, BLK, LANES),
        (4, NB, BLK, LANES),
        (3, NB, BLK, LANES),
        (3, NB, BLK, LANES),
    ]
    smem, vmem = pl.BlockSpec(memory_space=pltpu.SMEM), pl.BlockSpec(memory_space=pltpu.VMEM)
    return pl.pallas_call(
        functools.partial(kernel, steps),
        out_shape=jax.ShapeDtypeStruct(cotangent.shape, F32),
        in_specs=[smem, smem, smem, vmem, vmem, vmem, vmem, pl.BlockSpec(memory_space=pl.ANY)],
        out_specs=vmem,
        scratch_shapes=[pltpu.VMEM(shape, BF) for shape in shapes for _ in range(turns)]
        + [
            pltpu.VMEM((32, TPD, BLK, BLK), BF),
            pltpu.VMEM((NB, BLK, LANES), F32),
            pltpu.VMEM((NB * BLK, LANES), F32),
            pltpu.VMEM((NB * BLK, LANES), F32),
            pltpu.VMEM((3, 2, 32), jnp.int32),
            pltpu.SMEM((3, 2, 32), jnp.int32),
            pltpu.SMEM((128,), jnp.int32),
            pltpu.SemaphoreType.DMA((turns, SENDS)),
            pltpu.SemaphoreType.DMA((turns, ARRIVALS)),
            pltpu.SemaphoreType.DMA((2,)),
            pltpu.SemaphoreType.DMA((3,)),
            pltpu.SemaphoreType.DMA((3,)),
        ],
        compiler_params=pltpu.CompilerParams(collective_id=0, has_side_effects=True, vmem_limit_bytes=60 << 20),
    )(
        coeffs,
        pattern[0, 0].T,
        ask,
        cotangent,
        out_degree.reshape(NB, BLK),
        in_degree.reshape(NB, BLK),
        ask,
        tiles[0, 0],
    )


def solution(mesh):
    return jax.shard_map(
        on_device,
        mesh=mesh,
        in_specs=(
            P(("row", "col"), None),
            P(("row", "col")),
            P(("row", "col")),
            P(),
            P("row", "col", None, None, None, None),
            P("row", "col", None, None),
            P("row", "col", None, None),
        ),
        out_specs=P(("row", "col"), None),
        check_vma=False,
    )
```

```python
import functools

import jax
import jax.numpy as jnp
from jax import lax
from jax.experimental import pallas as pl
from jax.experimental.pallas import tpu as pltpu
from jax.sharding import PartitionSpec as P

MESH = pl.DeviceIdType.MESH
BF = jnp.bfloat16
F32 = jnp.float32
Y, Z, X = 4, 8, 4
BLK, NB, TPD, LANES = 128, 4, 4, 128
RA = 96
RB = BLK - RA
SENDS, ARRIVALS = 6, 21
EVENTS = 40
LEAD = 16
ORDERS = (
    "RgggggRRggggRgggRgggggggRgRRgnRRnnnnnRRR",
    "ggRgRgRgggRgggggRRgggnnnnRnRnRRgRR",
    "ngnnngnRnngnnnngngnngRnnRnggRngnngggRgnRngnnnngggnRnRgngRnRnRRn",
)
A1, PZ, SB, PY, A2, XX = 0, 7, 14, 18, 19, 20
KINDS = {A1: 0, PZ: 1, SB: 2, PY: 3, A2: 4, XX: 5}


def kernel(steps, coef, pat, req, cot, outd, ind, reqv, tiles_hbm, out, *scratch):
    turns = 2 * steps
    za, sa, pk, g1, ss, sr, xs, xr = (scratch[i * turns:(i + 1) * turns] for i in range(8))
    tiles, own, osc, isc, rqv, rqs, gix, ssem, rsem, lsem, qs, qr = scratch[8 * turns:]

    row, col = lax.axis_index("row"), lax.axis_index("col")
    y, z = row // Z, lax.rem(row, Z)
    x, k = col // 2, lax.rem(col, 2)

    def zat(n):
        return lax.rem(z + Z + n, Z)

    def at_z(n):
        return (y * Z + zat(n), col)

    def at_y(n):
        return (lax.rem(y + Y + n, Y) * Z + z, col)

    def at_x(n):
        return (row, lax.rem(x + X + n, X) * 2 + k)

    sibling = (row, x * 2 + 1 - k)
    yoff = (1, -1, 2)

    def remote(t, kind, n, src, dst, dev):
        return pltpu.make_async_remote_copy(
            src_ref=src,
            dst_ref=dst,
            send_sem=ssem.at[t, KINDS[kind]],
            recv_sem=rsem.at[t, kind + n],
            device_id=dev,
            device_id_type=MESH,
        )

    def send(t, kind, n, src, dst, dev):
        remote(t, kind, n, src, dst, dev).start()

    def arrived(t, kind, n, dst):
        remote(t, kind, n, dst, dst, sibling).wait_recv()

    def settle(t):
        for kind, ref in (
            (A1, za[t].at[pl.ds(0, Z - 1)]),
            (PZ, g1[t].at[pl.ds(0, (Z - 1) * Y * NB)]),
            (SB, ss[t]),
            (PY, g1[t].at[pl.ds(0, (Y - 1) * NB)]),
            (A2, pk[t]),
            (XX, xs[t]),
        ):
            remote(t, kind, 0, ref, ref, sibling).wait_send()

    load = pltpu.make_async_copy(tiles_hbm, tiles, lsem.at[0])
    load.start()

    barrier = pltpu.get_barrier_semaphore()
    peers = [at_z(1), at_z(-1), at_y(1), at_y(-1), at_y(2), at_x(1), at_x(-1), at_x(2), sibling]
    for peer in peers:
        pl.semaphore_signal(barrier, inc=1, device_id=peer, device_id_type=MESH)

    for i in range(NB):
        rows = pl.ds(i * BLK, BLK)
        osc[rows] = jnp.transpose(jnp.broadcast_to(lax.rsqrt(outd[i:i + 1].astype(F32)), (BLK, LANES)))
        isc[rows] = jnp.transpose(jnp.broadcast_to(lax.rsqrt(ind[i:i + 1].astype(F32)), (BLK, LANES)))

    pl.semaphore_wait(barrier, len(peers))

    asks = []
    for i, off in enumerate(yoff):
        ask = pltpu.make_async_remote_copy(
            src_ref=reqv, dst_ref=rqv.at[i], send_sem=qs.at[i], recv_sem=qr.at[i], device_id=at_y(-off), device_id_type=MESH
        )
        ask.start()
        asks.append(ask)

    placed = set()

    def place(t, i, value):
        placed.add(t)
        za[t][z, i] = value[:RA]
        g1[t][z * 16 + y * 4 + i] = value[RA:]

    def lanes(t):
        return pl.ds((t % 2) * LANES, LANES)

    def pack(t, e, zz):
        blocks = [za[t][zz, i] for i in range(NB)]
        slot = (y * Z + zz) * 2

        def chosen(r):
            return jnp.where(r == 0, blocks[0], jnp.where(r == 1, blocks[1], jnp.where(r == 2, blocks[2], blocks[3])))

        for i, off in enumerate(yoff):
            for s in range(2):
                pk[t][e, i, s] = chosen(rqs[i, s, y * Z + zz])
            send(t, A2, 0, pk[t].at[e, i], sa[t].at[pl.ds(slot, 2)], at_y(off))
        for s in range(2):
            sa[t][slot + s] = chosen(req[s, y * Z + zz])

    def whole(t, zz):
        return za[t].at[zz]

    def column(t, zz):
        return g1[t].at[pl.ds(zz * 16, 16)]

    def start(t):
        mine = g1[t].at[pl.ds(z * 16 + y * 4, 4)]
        send(t, A1, 0, whole(t, z), whole(t, z), at_z(1))
        send(t, A1, 1, whole(t, z), whole(t, z), at_z(-1))
        for i, off in enumerate(yoff):
            send(t, PY, 0, mine, mine, at_y(off))

    def gather(t):
        assert t in placed
        pack(t, 0, z)
        yield
        e = 1
        for hop in range(1, 5):
            if hop < 4:
                for d, sign in enumerate((-1, 1)):
                    zz = zat(sign * hop)
                    arrived(t, A1, 2 * hop - 2 + d, whole(t, zz))
                    if hop < 3:
                        part = whole(t, zz)
                    else:
                        part = za[t].at[zz, pl.ds(2 * d, 2)]
                    send(t, A1, min(2 * hop + d, 6), part, part, at_z(-sign))
                    yield
                for sign in (-1, 1):
                    pack(t, e, zat(sign * hop))
                    e += 1
                    if sign < 0:
                        yield
            else:
                zz = zat(4)
                arrived(t, A1, 6, whole(t, zz))
                pack(t, e, zz)
            yield
            if hop == 1:
                arrived(t, PY, 0, g1[t].at[pl.ds(0, (Y - 1) * NB)])
                for d, sign in enumerate((-1, 1)):
                    send(t, PZ, d, column(t, z), column(t, z), at_z(-sign))
            else:
                for d, sign in enumerate((-1, 1)):
                    zz = zat(sign * (hop - 1))
                    arrived(t, PZ, 2 * hop - 4 + d, column(t, zz))
                    if hop < 4:
                        part = column(t, zz)
                    else:
                        part = g1[t].at[pl.ds(zz * 16 + 8 * d, 8)]
                    send(t, PZ, min(2 * hop - 2 + d, 6), part, part, at_z(-sign))
                    if d == 0:
                        yield
            yield
        arrived(t, PZ, 6, column(t, zat(4)))
        yield
        arrived(t, A2, 0, sa[t].at[pl.ds(0, (Y - 1) * Z * 2)])

    def product(t, d):
        left = jnp.concatenate([tiles[d, j] for j in range(TPD)], axis=1)
        right = []
        for j in range(TPD):
            p = pat[j, d]
            right += [sa[t][p], g1[t][gix[d * TPD + j]]]
        return jnp.dot(left, jnp.concatenate(right, axis=0), preferred_element_type=F32)

    def reduce(t):
        def for_sibling(n, off):
            to = lax.rem(x + off, X) * 2 + 1 - k
            for i in range(NB):
                ss[t][n, i] = product(t, to * NB + i).astype(BF)
            send(t, SB, n, ss[t].at[n], sr[t].at[n], sibling)

        def for_x(n, off):
            to = lax.rem(x + off, X) * 2 + k
            sums = [product(t, to * NB + i) for i in range(NB)]
            arrived(t, SB, n, sr[t].at[n])
            for i in range(NB):
                xs[t][n, i] = (sums[i] + sr[t][n, i].astype(F32)).astype(BF)
            send(t, XX, 0, xs[t].at[n], xr[t].at[n], at_x(off))

        def first_two(n, carry):
            for_sibling(n, 2 - n)
            return carry

        def last_two(n, carry):
            for_sibling(n, 9 - 3 * n)
            return carry

        def neighbours(n, carry):
            for_x(n, 2 * n - 1)
            return carry

        lax.fori_loop(0, 2, first_two, 0)
        yield
        for_x(0, 2)
        yield
        lax.fori_loop(2, 4, last_two, 0)
        yield
        lax.fori_loop(1, 3, neighbours, 0)
        yield
        for i in range(NB):
            own[i] = product(t, col * NB + i)
        yield
        arrived(t, SB, 3, sr[t].at[3])
        arrived(t, XX, 0, xr[t])
        level = steps - 1 - t // 2
        for i in range(NB):
            rows = pl.ds(i * BLK, BLK)
            total = own[i] + sr[t][3, i].astype(F32)
            for n in range(3):
                total = total + xr[t][n, i].astype(F32)
            h = isc[rows] * total + coef[level] * cot[rows, lanes(t)]
            if level == 0:
                out[rows, lanes(t)] = h
            else:
                place(t + 2, i, (osc[rows] * h).astype(BF))
        if level > 0:
            start(t + 2)
        yield

    for t in range(2):
        for i in range(NB):
            rows = pl.ds(i * BLK, BLK)
            place(t, i, (osc[rows] * (coef[steps] * cot[rows, lanes(t)])).astype(BF))
        if t == 0:
            start(t)

    def slot_of(i, carry):
        for j in range(TPD):
            p = pat[j, i]
            gix[i * TPD + j] = ((p // 2 % Z) * Y + p // 16) * NB + req[p % 2, p // 2]
        return carry

    lax.fori_loop(0, pat.shape[1], slot_of, 0)
    for ask in asks:
        ask.wait()
    to_scalar = pltpu.make_async_copy(rqv, rqs, lsem.at[1])
    to_scalar.start()
    to_scalar.wait()

    def run(events, count):
        for _ in range(count):
            next(events, None)

    gathers = {t: gather(t) for t in range(turns)}
    run(gathers[0], LEAD)
    start(1)
    run(gathers[0], EVENTS)
    load.wait()
    for t in range(1, turns + 1):
        streams = {"R": reduce(t - 1), "g": gathers.get(t, iter(())), "n": gathers.get(t + 1, iter(()))}
        for letter in ORDERS[0 if t == 1 else 1 if t < turns - 1 else 2]:
            run(streams[letter], 1)
        run(streams["R"], EVENTS)
        run(streams["g"], EVENTS)
        settle(t - 1)


def on_device(cotangent, out_degree, in_degree, coeffs, tiles, pattern, requests):
    steps = coeffs.shape[0] - 1
    turns = 2 * steps
    ask = requests[0, 0].T
    shapes = [
        (Z, NB, RA, LANES),
        (Y * Z * 2, RA, LANES),
        (Z, 3, 2, RA, LANES),
        (Y * Z * NB, RB, LANES),
        (4, NB, BLK, LANES),
        (4, NB, BLK, LANES),
        (3, NB, BLK, LANES),
        (3, NB, BLK, LANES),
    ]
    smem, vmem = pl.BlockSpec(memory_space=pltpu.SMEM), pl.BlockSpec(memory_space=pltpu.VMEM)
    return pl.pallas_call(
        functools.partial(kernel, steps),
        out_shape=jax.ShapeDtypeStruct(cotangent.shape, F32),
        in_specs=[smem, smem, smem, vmem, vmem, vmem, vmem, pl.BlockSpec(memory_space=pl.ANY)],
        out_specs=vmem,
        scratch_shapes=[pltpu.VMEM(shape, BF) for shape in shapes for _ in range(turns)]
        + [
            pltpu.VMEM((32, TPD, BLK, BLK), BF),
            pltpu.VMEM((NB, BLK, LANES), F32),
            pltpu.VMEM((NB * BLK, LANES), F32),
            pltpu.VMEM((NB * BLK, LANES), F32),
            pltpu.VMEM((3, 2, 32), jnp.int32),
            pltpu.SMEM((3, 2, 32), jnp.int32),
            pltpu.SMEM((128,), jnp.int32),
            pltpu.SemaphoreType.DMA((turns, SENDS)),
            pltpu.SemaphoreType.DMA((turns, ARRIVALS)),
            pltpu.SemaphoreType.DMA((2,)),
            pltpu.SemaphoreType.DMA((3,)),
            pltpu.SemaphoreType.DMA((3,)),
        ],
        compiler_params=pltpu.CompilerParams(collective_id=0, has_side_effects=True, vmem_limit_bytes=60 << 20),
    )(
        coeffs,
        pattern[0, 0].T,
        ask,
        cotangent,
        out_degree.reshape(NB, BLK),
        in_degree.reshape(NB, BLK),
        ask,
        tiles[0, 0],
    )


def solution(mesh):
    return jax.shard_map(
        on_device,
        mesh=mesh,
        in_specs=(
            P(("row", "col"), None),
            P(("row", "col")),
            P(("row", "col")),
            P(),
            P("row", "col", None, None, None, None),
            P("row", "col", None, None),
            P("row", "col", None, None),
        ),
        out_specs=P(("row", "col"), None),
        check_vma=False,
    )
```

```python
import functools

import jax
import jax.numpy as jnp
from jax import lax
from jax.experimental import pallas as pl
from jax.experimental.pallas import tpu as pltpu
from jax.sharding import PartitionSpec as P

MESH = pl.DeviceIdType.MESH
BF = jnp.bfloat16
F32 = jnp.float32
Y, Z, X = 4, 8, 4
BLK, NB, TPD, LANES = 128, 4, 4, 128
RA = 96
RB = BLK - RA
SENDS, ARRIVALS = 6, 21
EVENTS = 40
LEAD = 7
ORDERS = (
    "RggggRgRggRggggRggggRgnRgggnnnngnR",
    "RRggRgRggggRgggggRgnRggnRnnnn",
    "RnRgRggngRggggggngRgnnRnngngnnnnR",
)
A1, PZ, SB, PY, A2, XX = 0, 7, 14, 18, 19, 20
KINDS = {A1: 0, PZ: 1, SB: 2, PY: 3, A2: 4, XX: 5}


def kernel(steps, coef, pat, req, cot, outd, ind, reqv, tiles_hbm, out, *scratch):
    turns = 2 * steps
    za, sa, pk, g1, ss, sr, xs, xr = (scratch[i * turns:(i + 1) * turns] for i in range(8))
    tiles, own, osc, isc, rqv, rqs, gix, ssem, rsem, lsem, qs, qr = scratch[8 * turns:]

    row, col = lax.axis_index("row"), lax.axis_index("col")
    y, z = row // Z, lax.rem(row, Z)
    x, k = col // 2, lax.rem(col, 2)

    def zat(n):
        return lax.rem(z + Z + n, Z)

    def at_z(n):
        return (y * Z + zat(n), col)

    def at_y(n):
        return (lax.rem(y + Y + n, Y) * Z + z, col)

    def at_x(n):
        return (row, lax.rem(x + X + n, X) * 2 + k)

    sibling = (row, x * 2 + 1 - k)
    yoff = (1, -1, 2)

    def remote(t, kind, n, src, dst, dev):
        return pltpu.make_async_remote_copy(
            src_ref=src,
            dst_ref=dst,
            send_sem=ssem.at[t, KINDS[kind]],
            recv_sem=rsem.at[t, kind + n],
            device_id=dev,
            device_id_type=MESH,
        )

    def send(t, kind, n, src, dst, dev):
        remote(t, kind, n, src, dst, dev).start()

    def arrived(t, kind, n, dst):
        remote(t, kind, n, dst, dst, sibling).wait_recv()

    def settle(t):
        for kind, ref in (
            (A1, za[t].at[pl.ds(0, Z - 1)]),
            (PZ, g1[t].at[pl.ds(0, (Z - 1) * Y * NB)]),
            (SB, ss[t]),
            (PY, g1[t].at[pl.ds(0, (Y - 1) * NB)]),
            (A2, pk[t]),
            (XX, xs[t]),
        ):
            remote(t, kind, 0, ref, ref, sibling).wait_send()

    load = pltpu.make_async_copy(tiles_hbm, tiles, lsem.at[0])
    load.start()

    barrier = pltpu.get_barrier_semaphore()
    peers = [at_z(1), at_z(-1), at_y(1), at_y(-1), at_y(2), at_x(1), at_x(-1), at_x(2), sibling]
    for peer in peers:
        pl.semaphore_signal(barrier, inc=1, device_id=peer, device_id_type=MESH)

    for i in range(NB):
        rows = pl.ds(i * BLK, BLK)
        osc[rows] = jnp.transpose(jnp.broadcast_to(lax.rsqrt(outd[i:i + 1].astype(F32)), (BLK, LANES)))
        isc[rows] = jnp.transpose(jnp.broadcast_to(lax.rsqrt(ind[i:i + 1].astype(F32)), (BLK, LANES)))

    pl.semaphore_wait(barrier, len(peers))

    asks = []
    for i, off in enumerate(yoff):
        ask = pltpu.make_async_remote_copy(
            src_ref=reqv, dst_ref=rqv.at[i], send_sem=qs.at[i], recv_sem=qr.at[i], device_id=at_y(-off), device_id_type=MESH
        )
        ask.start()
        asks.append(ask)

    placed = set()

    def place(t, i, value):
        placed.add(t)
        za[t][z, i] = value[:RA]
        g1[t][z * 16 + y * 4 + i] = value[RA:]

    def lanes(t):
        return pl.ds((t % 2) * LANES, LANES)

    def pack(t, e, zz):
        blocks = [za[t][zz, i] for i in range(NB)]
        slot = (y * Z + zz) * 2

        def chosen(r):
            return jnp.where(r == 0, blocks[0], jnp.where(r == 1, blocks[1], jnp.where(r == 2, blocks[2], blocks[3])))

        for i, off in enumerate(yoff):
            for s in range(2):
                pk[t][e, i, s] = chosen(rqs[i, s, y * Z + zz])
            send(t, A2, 0, pk[t].at[e, i], sa[t].at[pl.ds(slot, 2)], at_y(off))
        for s in range(2):
            sa[t][slot + s] = chosen(req[s, y * Z + zz])

    def whole(t, zz):
        return za[t].at[zz]

    def column(t, zz):
        return g1[t].at[pl.ds(zz * 16, 16)]

    def start(t):
        mine = g1[t].at[pl.ds(z * 16 + y * 4, 4)]
        send(t, A1, 0, whole(t, z), whole(t, z), at_z(1))
        send(t, A1, 1, whole(t, z), whole(t, z), at_z(-1))
        for i, off in enumerate(yoff):
            send(t, PY, 0, mine, mine, at_y(off))

    def gather(t):
        assert t in placed
        pack(t, 0, z)
        yield
        e = 1
        for hop in range(1, 5):
            if hop < 4:
                for d, sign in enumerate((-1, 1)):
                    zz = zat(sign * hop)
                    arrived(t, A1, 2 * hop - 2 + d, whole(t, zz))
                    if hop < 3:
                        part = whole(t, zz)
                    else:
                        part = za[t].at[zz, pl.ds(2 * d, 2)]
                    send(t, A1, min(2 * hop + d, 6), part, part, at_z(-sign))
                    yield
                for sign in (-1, 1):
                    pack(t, e, zat(sign * hop))
                    e += 1
                    if sign < 0:
                        yield
            else:
                zz = zat(4)
                arrived(t, A1, 6, whole(t, zz))
                pack(t, e, zz)
            yield
            if hop == 1:
                arrived(t, PY, 0, g1[t].at[pl.ds(0, (Y - 1) * NB)])
                for d, sign in enumerate((-1, 1)):
                    send(t, PZ, d, column(t, z), column(t, z), at_z(-sign))
            else:
                for d, sign in enumerate((-1, 1)):
                    zz = zat(sign * (hop - 1))
                    arrived(t, PZ, 2 * hop - 4 + d, column(t, zz))
                    if hop < 4:
                        part = column(t, zz)
                    else:
                        part = g1[t].at[pl.ds(zz * 16 + 8 * d, 8)]
                    send(t, PZ, min(2 * hop - 2 + d, 6), part, part, at_z(-sign))
                    if d == 0:
                        yield
            yield
        arrived(t, PZ, 6, column(t, zat(4)))
        yield
        arrived(t, A2, 0, sa[t].at[pl.ds(0, (Y - 1) * Z * 2)])

    def product(t, d):
        left = jnp.concatenate([tiles[d, j] for j in range(TPD)], axis=1)
        right = []
        for j in range(TPD):
            p = pat[j, d]
            right += [sa[t][p], g1[t][gix[d * TPD + j]]]
        return jnp.dot(left, jnp.concatenate(right, axis=0), preferred_element_type=F32)

    def reduce(t):
        def for_sibling(n, off):
            to = lax.rem(x + off, X) * 2 + 1 - k
            for i in range(NB):
                ss[t][n, i] = product(t, to * NB + i).astype(BF)
            send(t, SB, n, ss[t].at[n], sr[t].at[n], sibling)

        def for_x(n, off):
            to = lax.rem(x + off, X) * 2 + k
            sums = [product(t, to * NB + i) for i in range(NB)]
            arrived(t, SB, n, sr[t].at[n])
            for i in range(NB):
                xs[t][n, i] = (sums[i] + sr[t][n, i].astype(F32)).astype(BF)
            send(t, XX, 0, xs[t].at[n], xr[t].at[n], at_x(off))

        def first_two(n, carry):
            for_sibling(n, 2 - n)
            return carry

        def last_two(n, carry):
            for_sibling(n, 9 - 3 * n)
            return carry

        def neighbours(n, carry):
            for_x(n, 2 * n - 1)
            return carry

        lax.fori_loop(0, 2, first_two, 0)
        yield
        for_x(0, 2)
        yield
        lax.fori_loop(2, 4, last_two, 0)
        yield
        lax.fori_loop(1, 3, neighbours, 0)
        yield
        for i in range(NB):
            own[i] = product(t, col * NB + i)
        yield
        arrived(t, SB, 3, sr[t].at[3])
        arrived(t, XX, 0, xr[t])
        level = steps - 1 - t // 2
        for i in range(NB):
            rows = pl.ds(i * BLK, BLK)
            total = own[i] + sr[t][3, i].astype(F32)
            for n in range(3):
                total = total + xr[t][n, i].astype(F32)
            h = isc[rows] * total + coef[level] * cot[rows, lanes(t)]
            if level == 0:
                out[rows, lanes(t)] = h
            else:
                place(t + 2, i, (osc[rows] * h).astype(BF))
        if level > 0:
            start(t + 2)
        yield

    for t in range(2):
        for i in range(NB):
            rows = pl.ds(i * BLK, BLK)
            place(t, i, (osc[rows] * (coef[steps] * cot[rows, lanes(t)])).astype(BF))
        if t == 0:
            start(t)

    def slot_of(i, carry):
        for j in range(TPD):
            p = pat[j, i]
            gix[i * TPD + j] = ((p // 2 % Z) * Y + p // 16) * NB + req[p % 2, p // 2]
        return carry

    lax.fori_loop(0, pat.shape[1], slot_of, 0)
    for ask in asks:
        ask.wait()
    to_scalar = pltpu.make_async_copy(rqv, rqs, lsem.at[1])
    to_scalar.start()
    to_scalar.wait()

    def run(events, count):
        for _ in range(count):
            next(events, None)

    gathers = {t: gather(t) for t in range(turns)}
    run(gathers[0], LEAD)
    start(1)
    run(gathers[0], EVENTS)
    load.wait()
    for t in range(1, turns + 1):
        streams = {"R": reduce(t - 1), "g": gathers.get(t, iter(())), "n": gathers.get(t + 1, iter(()))}
        for letter in ORDERS[0 if t == 1 else 1 if t < turns - 1 else 2]:
            run(streams[letter], 1)
        run(streams["R"], EVENTS)
        run(streams["g"], EVENTS)
        settle(t - 1)


def on_device(cotangent, out_degree, in_degree, coeffs, tiles, pattern, requests):
    steps = coeffs.shape[0] - 1
    turns = 2 * steps
    ask = requests[0, 0].T
    shapes = [
        (Z, NB, RA, LANES),
        (Y * Z * 2, RA, LANES),
        (Z, 3, 2, RA, LANES),
        (Y * Z * NB, RB, LANES),
        (4, NB, BLK, LANES),
        (4, NB, BLK, LANES),
        (3, NB, BLK, LANES),
        (3, NB, BLK, LANES),
    ]
    smem, vmem = pl.BlockSpec(memory_space=pltpu.SMEM), pl.BlockSpec(memory_space=pltpu.VMEM)
    return pl.pallas_call(
        functools.partial(kernel, steps),
        out_shape=jax.ShapeDtypeStruct(cotangent.shape, F32),
        in_specs=[smem, smem, smem, vmem, vmem, vmem, vmem, pl.BlockSpec(memory_space=pltpu.HBM)],
        out_specs=vmem,
        scratch_shapes=[pltpu.VMEM(shape, BF) for shape in shapes for _ in range(turns)]
        + [
            pltpu.VMEM((32, TPD, BLK, BLK), BF),
            pltpu.VMEM((NB, BLK, LANES), F32),
            pltpu.VMEM((NB * BLK, LANES), F32),
            pltpu.VMEM((NB * BLK, LANES), F32),
            pltpu.VMEM((3, 2, 32), jnp.int32),
            pltpu.SMEM((3, 2, 32), jnp.int32),
            pltpu.SMEM((128,), jnp.int32),
            pltpu.SemaphoreType.DMA((turns, SENDS)),
            pltpu.SemaphoreType.DMA((turns, ARRIVALS)),
            pltpu.SemaphoreType.DMA((2,)),
            pltpu.SemaphoreType.DMA((3,)),
            pltpu.SemaphoreType.DMA((3,)),
        ],
        compiler_params=pltpu.CompilerParams(collective_id=0, has_side_effects=True, vmem_limit_bytes=49 << 20),
    )(
        coeffs,
        pattern[0, 0].T,
        ask,
        cotangent,
        out_degree.reshape(NB, BLK),
        in_degree.reshape(NB, BLK),
        ask,
        tiles[0, 0],
    )


def solution(mesh):
    return jax.shard_map(
        on_device,
        mesh=mesh,
        in_specs=(
            P(("row", "col"), None),
            P(("row", "col")),
            P(("row", "col")),
            P(),
            P("row", "col", None, None, None, None),
            P("row", "col", None, None),
            P("row", "col", None, None),
        ),
        out_specs=P(("row", "col"), None),
        check_vma=False,
    )
```

```python
import functools

import jax
import jax.numpy as jnp
from jax import lax
from jax.experimental import pallas as pl
from jax.experimental.pallas import tpu as pltpu
from jax.sharding import PartitionSpec as P

MESH = pl.DeviceIdType.MESH
BF = jnp.bfloat16
F32 = jnp.float32
Y, Z, X = 4, 8, 4
BLK, NB, TPD, LANES = 128, 4, 4, 128
RA = 96
RB = BLK - RA
SENDS, ARRIVALS = 6, 21
EVENTS = 40
LEAD = 7
ORDERS = (
    "RggggRgRggRggggRggggRgnRgggnnnngnR",
    "RRggRgRggggRgggggRgnRggnRnnnn",
    "RnRgRggngRggggggngRgnnRnngngnnnnR",
)
A1, PZ, SB, PY, A2, XX = 0, 7, 14, 18, 19, 20
KINDS = {A1: 0, PZ: 1, SB: 2, PY: 3, A2: 4, XX: 5}


def kernel(steps, coef, pat, req, cot, outd, ind, reqv, tiles_hbm, out, *scratch):
    turns = 2 * steps
    za, sa, pk, g1, ss, sr, xs, xr = (scratch[i * turns:(i + 1) * turns] for i in range(8))
    tiles, own, osc, isc, rqv, rqs, gix, ssem, rsem, lsem, qs, qr = scratch[8 * turns:]

    row, col = lax.axis_index("row"), lax.axis_index("col")
    y, z = row // Z, lax.rem(row, Z)
    x, k = col // 2, lax.rem(col, 2)

    def zat(n):
        return lax.rem(z + Z + n, Z)

    def at_z(n):
        return (y * Z + zat(n), col)

    def at_y(n):
        return (lax.rem(y + Y + n, Y) * Z + z, col)

    def at_x(n):
        return (row, lax.rem(x + X + n, X) * 2 + k)

    sibling = (row, x * 2 + 1 - k)
    yoff = (2, 1, -1)

    def remote(t, kind, n, src, dst, dev):
        return pltpu.make_async_remote_copy(
            src_ref=src,
            dst_ref=dst,
            send_sem=ssem.at[t, KINDS[kind]],
            recv_sem=rsem.at[t, kind + n],
            device_id=dev,
            device_id_type=MESH,
        )

    def send(t, kind, n, src, dst, dev):
        remote(t, kind, n, src, dst, dev).start()

    def arrived(t, kind, n, dst):
        remote(t, kind, n, dst, dst, sibling).wait_recv()

    def settle(t):
        for kind, ref in (
            (A1, za[t].at[pl.ds(0, Z - 1)]),
            (PZ, g1[t].at[pl.ds(0, (Z - 1) * Y * NB)]),
            (SB, ss[t]),
            (PY, g1[t].at[pl.ds(0, (Y - 1) * NB)]),
            (A2, pk[t]),
            (XX, xs[t]),
        ):
            remote(t, kind, 0, ref, ref, sibling).wait_send()

    load = pltpu.make_async_copy(tiles_hbm, tiles, lsem.at[0])
    load.start()

    barrier = pltpu.get_barrier_semaphore()
    peers = [at_z(1), at_z(-1), at_y(1), at_y(-1), at_y(2), at_x(1), at_x(-1), at_x(2), sibling]
    for peer in peers:
        pl.semaphore_signal(barrier, inc=1, device_id=peer, device_id_type=MESH)

    for i in range(NB):
        rows = pl.ds(i * BLK, BLK)
        osc[rows] = jnp.transpose(jnp.broadcast_to(lax.rsqrt(outd[i:i + 1].astype(F32)), (BLK, LANES)))
        isc[rows] = jnp.transpose(jnp.broadcast_to(lax.rsqrt(ind[i:i + 1].astype(F32)), (BLK, LANES)))

    pl.semaphore_wait(barrier, len(peers))

    asks = []
    for i, off in enumerate(yoff):
        ask = pltpu.make_async_remote_copy(
            src_ref=reqv, dst_ref=rqv.at[i], send_sem=qs.at[i], recv_sem=qr.at[i], device_id=at_y(-off), device_id_type=MESH
        )
        ask.start()
        asks.append(ask)

    placed = set()

    def place(t, i, value):
        placed.add(t)
        za[t][z, i] = value[:RA]
        g1[t][z * 16 + y * 4 + i] = value[RA:]

    def lanes(t):
        return pl.ds((t % 2) * LANES, LANES)

    def pack(t, e, zz):
        blocks = [za[t][zz, i] for i in range(NB)]
        slot = (y * Z + zz) * 2

        def chosen(r):
            return jnp.where(r == 0, blocks[0], jnp.where(r == 1, blocks[1], jnp.where(r == 2, blocks[2], blocks[3])))

        for i, off in enumerate(yoff):
            for s in range(2):
                pk[t][e, i, s] = chosen(rqs[i, s, y * Z + zz])
            send(t, A2, 0, pk[t].at[e, i], sa[t].at[pl.ds(slot, 2)], at_y(off))
        for s in range(2):
            sa[t][slot + s] = chosen(req[s, y * Z + zz])

    def whole(t, zz):
        return za[t].at[zz]

    def column(t, zz):
        return g1[t].at[pl.ds(zz * 16, 16)]

    def start(t):
        mine = g1[t].at[pl.ds(z * 16 + y * 4, 4)]
        send(t, A1, 0, whole(t, z), whole(t, z), at_z(1))
        send(t, A1, 1, whole(t, z), whole(t, z), at_z(-1))
        for i, off in enumerate(yoff):
            send(t, PY, 0, mine, mine, at_y(off))

    def gather(t):
        assert t in placed
        pack(t, 0, z)
        yield
        e = 1
        for hop in range(1, 5):
            if hop < 4:
                for d, sign in enumerate((-1, 1)):
                    zz = zat(sign * hop)
                    arrived(t, A1, 2 * hop - 2 + d, whole(t, zz))
                    if hop < 3:
                        part = whole(t, zz)
                    else:
                        part = za[t].at[zz, pl.ds(2 * d, 2)]
                    send(t, A1, min(2 * hop + d, 6), part, part, at_z(-sign))
                    yield
                for sign in (-1, 1):
                    pack(t, e, zat(sign * hop))
                    e += 1
                    if sign < 0:
                        yield
            else:
                zz = zat(4)
                arrived(t, A1, 6, whole(t, zz))
                pack(t, e, zz)
            yield
            if hop == 1:
                arrived(t, PY, 0, g1[t].at[pl.ds(0, (Y - 1) * NB)])
                for d, sign in enumerate((-1, 1)):
                    send(t, PZ, d, column(t, z), column(t, z), at_z(-sign))
            else:
                for d, sign in enumerate((-1, 1)):
                    zz = zat(sign * (hop - 1))
                    arrived(t, PZ, 2 * hop - 4 + d, column(t, zz))
                    if hop < 4:
                        part = column(t, zz)
                    else:
                        part = g1[t].at[pl.ds(zz * 16 + 8 * d, 8)]
                    send(t, PZ, min(2 * hop - 2 + d, 6), part, part, at_z(-sign))
                    if d == 0:
                        yield
            yield
        arrived(t, PZ, 6, column(t, zat(4)))
        yield
        arrived(t, A2, 0, sa[t].at[pl.ds(0, (Y - 1) * Z * 2)])

    def product(t, d):
        left = jnp.concatenate([tiles[d, j] for j in range(TPD)], axis=1)
        right = []
        for j in range(TPD):
            p = pat[j, d]
            right += [sa[t][p], g1[t][gix[d * TPD + j]]]
        return jnp.dot(left, jnp.concatenate(right, axis=0), preferred_element_type=F32)

    def reduce(t):
        def for_sibling(n, off):
            to = lax.rem(x + off, X) * 2 + 1 - k
            for i in range(NB):
                ss[t][n, i] = product(t, to * NB + i).astype(BF)
            send(t, SB, n, ss[t].at[n], sr[t].at[n], sibling)

        def for_x(n, off):
            to = lax.rem(x + off, X) * 2 + k
            sums = [product(t, to * NB + i) for i in range(NB)]
            arrived(t, SB, n, sr[t].at[n])
            for i in range(NB):
                xs[t][n, i] = (sums[i] + sr[t][n, i].astype(F32)).astype(BF)
            send(t, XX, 0, xs[t].at[n], xr[t].at[n], at_x(off))

        def first_two(n, carry):
            for_sibling(n, 2 - n)
            return carry

        def last_two(n, carry):
            for_sibling(n, 9 - 3 * n)
            return carry

        def neighbours(n, carry):
            for_x(n, 2 * n - 1)
            return carry

        lax.fori_loop(0, 2, first_two, 0)
        yield
        for_x(0, 2)
        yield
        lax.fori_loop(2, 4, last_two, 0)
        yield
        lax.fori_loop(1, 3, neighbours, 0)
        yield
        for i in range(NB):
            own[i] = product(t, col * NB + i)
        yield
        arrived(t, SB, 3, sr[t].at[3])
        arrived(t, XX, 0, xr[t])
        level = steps - 1 - t // 2
        for i in range(NB):
            rows = pl.ds(i * BLK, BLK)
            total = own[i] + sr[t][3, i].astype(F32)
            for n in range(3):
                total = total + xr[t][n, i].astype(F32)
            h = isc[rows] * total + coef[level] * cot[rows, lanes(t)]
            if level == 0:
                out[rows, lanes(t)] = h
            else:
                place(t + 2, i, (osc[rows] * h).astype(BF))
        if level > 0:
            start(t + 2)
        yield

    for t in range(2):
        for i in range(NB):
            rows = pl.ds(i * BLK, BLK)
            place(t, i, (osc[rows] * (coef[steps] * cot[rows, lanes(t)])).astype(BF))
        if t == 0:
            start(t)

    def slot_of(i, carry):
        for j in range(TPD):
            p = pat[j, i]
            gix[i * TPD + j] = ((p // 2 % Z) * Y + p // 16) * NB + req[p % 2, p // 2]
        return carry

    lax.fori_loop(0, pat.shape[1], slot_of, 0)
    for ask in asks:
        ask.wait()
    to_scalar = pltpu.make_async_copy(rqv, rqs, lsem.at[1])
    to_scalar.start()
    to_scalar.wait()

    def run(events, count):
        for _ in range(count):
            next(events, None)

    gathers = {t: gather(t) for t in range(turns)}
    run(gathers[0], LEAD)
    start(1)
    run(gathers[0], EVENTS)
    load.wait()
    for t in range(1, turns + 1):
        streams = {"R": reduce(t - 1), "g": gathers.get(t, iter(())), "n": gathers.get(t + 1, iter(()))}
        for letter in ORDERS[0 if t == 1 else 1 if t < turns - 1 else 2]:
            run(streams[letter], 1)
        run(streams["R"], EVENTS)
        run(streams["g"], EVENTS)
        settle(t - 1)


def on_device(cotangent, out_degree, in_degree, coeffs, tiles, pattern, requests):
    steps = coeffs.shape[0] - 1
    turns = 2 * steps
    ask = requests[0, 0].T
    shapes = [
        (Z, NB, RA, LANES),
        (Y * Z * 2, RA, LANES),
        (Z, 3, 2, RA, LANES),
        (Y * Z * NB, RB, LANES),
        (4, NB, BLK, LANES),
        (4, NB, BLK, LANES),
        (3, NB, BLK, LANES),
        (3, NB, BLK, LANES),
    ]
    smem, vmem = pl.BlockSpec(memory_space=pltpu.SMEM), pl.BlockSpec(memory_space=pltpu.VMEM)
    return pl.pallas_call(
        functools.partial(kernel, steps),
        out_shape=jax.ShapeDtypeStruct(cotangent.shape, F32),
        in_specs=[smem, smem, smem, vmem, vmem, vmem, vmem, pl.BlockSpec(memory_space=pl.ANY)],
        out_specs=vmem,
        scratch_shapes=[pltpu.VMEM(shape, BF) for shape in shapes for _ in range(turns)]
        + [
            pltpu.VMEM((32, TPD, BLK, BLK), BF),
            pltpu.VMEM((NB, BLK, LANES), F32),
            pltpu.VMEM((NB * BLK, LANES), F32),
            pltpu.VMEM((NB * BLK, LANES), F32),
            pltpu.VMEM((3, 2, 32), jnp.int32),
            pltpu.SMEM((3, 2, 32), jnp.int32),
            pltpu.SMEM((128,), jnp.int32),
            pltpu.SemaphoreType.DMA((turns, SENDS)),
            pltpu.SemaphoreType.DMA((turns, ARRIVALS)),
            pltpu.SemaphoreType.DMA((2,)),
            pltpu.SemaphoreType.DMA((3,)),
            pltpu.SemaphoreType.DMA((3,)),
        ],
        compiler_params=pltpu.CompilerParams(collective_id=0, has_side_effects=True, vmem_limit_bytes=60 << 20),
    )(
        coeffs,
        pattern[0, 0].T,
        ask,
        cotangent,
        out_degree.reshape(NB, BLK),
        in_degree.reshape(NB, BLK),
        ask,
        tiles[0, 0],
    )


def solution(mesh):
    return jax.shard_map(
        on_device,
        mesh=mesh,
        in_specs=(
            P(("row", "col"), None),
            P(("row", "col")),
            P(("row", "col")),
            P(),
            P("row", "col", None, None, None, None),
            P("row", "col", None, None),
            P("row", "col", None, None),
        ),
        out_specs=P(("row", "col"), None),
        check_vma=False,
    )
```
